32 devices in a mesh: dp: 16 (over z, x, core), mp: 2 (over y).
Axes of the slice: x: 2, y: 2, z: 4, core: 2. Of those that a mesh axis runs over, the one named last changes fastest.
Arguments:
- features: bfloat16 [2, 8192, 768], P(None, 'dp', 'mp'), may hold values from -6 to 6
- proj_weight: bfloat16 [768, 1024], P('mp'), may hold values from -0.21875 to 0.21875
- bias_first: float32 [1024], replicated, may hold values from -3 to 3
- self_weight: bfloat16 [1024, 153], replicated, may hold values from -27 to 27
- neigh_weight: bfloat16 [1024, 153], replicated, may hold values from -0.1875 to 0.1875
- first_neighbours: int32 [2, 2048, 10], P(None, ('dp', 'mp')), may hold values from 0 to 255
- first_counts: int32 [2, 2048], P(None, ('dp', 'mp')), may hold values from 1 to 10
- second_neighbours: int32 [2, 512, 10], P(None, ('dp', 'mp')), may hold values from 0 to 63
- second_counts: int32 [2, 512], P(None, ('dp', 'mp')), may hold values from 1 to 10
- labels: int32 [2, 512], P(None, ('dp', 'mp')), may hold values from 0 to 152
Outputs:
- grad_proj: float32 [768, 1024], P('mp')
- grad_self: float32 [1024, 153], replicated
- grad_neigh: float32 [1024, 153], replicated
- grad_bias: float32 [1024], replicated
The draws below stay inside these ranges and needn't reach their ends.
All inputs are finite; a program needn't handle non-finite values.
Results may differ from the reference program's by a relative error of at most 0.011.
Values may be sent and summed in bfloat16 or wider, within the bound.
A program may use at most 64 MiB of HBM per device.

```python
import math
import jax
import jax.numpy as jnp
from jax import lax

F = 768
D = 1024
CLS = 153
FAN = 10
MB = 2
LOC = 256
MID = 64
TGT = 16
ROWS = 8192
N_DP = 16
N_MP = 2


def draw_self_weight(key, part):
    key = jax.random.fold_in(key, 11)
    values = jnp.clip(jax.random.normal(jax.random.fold_in(key, 1), (D, CLS), jnp.float32), -6.0, 6.0) / jnp.sqrt(jnp.float32(D))
    return values.astype(jnp.bfloat16)


def place_ends(result, rng, low, largest):
    place = [jax.random.randint(jax.random.fold_in(rng, axis), (), 0, length) for axis, length in enumerate(result.shape)]
    widest = result.shape.index(max(result.shape))
    neighbour = place[:widest] + [(place[widest] + 1) % result.shape[widest]] + place[widest + 1:]
    return result.at[tuple(place)].set(low).at[tuple(neighbour)].set(largest)


def level_of(key, shape, pieces, smallest, top_value):
    factor_of = 1.0
    for axis_at, blocks in pieces:
        draws = jax.random.uniform(jax.random.fold_in(jax.random.fold_in(key, 6), axis_at), (blocks,), jnp.float32, smallest / len(pieces), top_value / len(pieces))
        factor_of = factor_of * jnp.repeat(jnp.exp(draws), shape[axis_at] // blocks).reshape((-1,) + (1,) * (len(shape) - 1 - axis_at))
    return factor_of


def centred(key, shape, scale, reach, shards=(), kind=jnp.bfloat16):
    array = jax.random.normal(key, shape, jnp.float32) * scale
    if len(shards) > 0:
        array = level_of(key, shape, shards, -0.22, 0.18) * array
    return jnp.clip(array, min=-reach, max=reach).astype(kind)


def setup_inputs(seed: int = 0) -> dict:
    splits = jax.random.split(jax.random.key(seed), 11)
    return {
        "features": centred(splits[0], (MB, ROWS, F), 1.0, 6.0, ((1, 16), (2, 2))),
        "proj_weight": centred(splits[1], (F, D), F ** -0.5, 0.21875, ((0, 2),)),
        "bias_first": centred(splits[2], (D,), 0.5, 3.0, (), jnp.float32),
        "self_weight": draw_self_weight(jax.random.fold_in(splits[10], 71), 0),
        "neigh_weight": centred(splits[4], (D, CLS), D ** -0.5, 0.1875),
        "first_neighbours": place_ends(jax.random.randint(splits[5], (MB, N_DP * N_MP * MID, FAN), 0, LOC), jax.random.fold_in(splits[5], 1), 0, LOC - 1).astype(jnp.int32),
        "first_counts": place_ends(jax.random.randint(splits[6], (MB, N_DP * N_MP * MID), 1, FAN + 1), jax.random.fold_in(splits[6], 1), 1, FAN).astype(jnp.int32),
        "second_neighbours": place_ends(jax.random.randint(splits[7], (MB, N_DP * N_MP * TGT, FAN), 0, MID), jax.random.fold_in(splits[7], 1), 0, MID - 1).astype(jnp.int32),
        "second_counts": place_ends(jax.random.randint(splits[8], (MB, N_DP * N_MP * TGT), 1, FAN + 1), jax.random.fold_in(splits[8], 1), 1, FAN).astype(jnp.int32),
        "labels": place_ends(jax.random.randint(splits[9], (MB, N_DP * N_MP * TGT), 0, CLS), jax.random.fold_in(splits[9], 1), 0, CLS - 1).astype(jnp.int32),
    }


def sage_block(projected, bias_first, self_weight, neigh_weight, first_neighbours, first_counts, second_neighbours, second_counts, labels, scale):
    inner = first_neighbours.shape[0]
    target = second_neighbours.shape[0]
    fanout = first_neighbours.shape[1]
    classes = self_weight.shape[1]
    columns = jnp.arange(fanout, dtype=jnp.int32)
    first_inv = 1.0 / (first_counts.astype(jnp.float32) + 1.0)
    first_mix = jnp.where(columns[None, :] < first_counts[:, None], first_inv[:, None], 0.0).astype(jnp.float32)
    pre_act = bias_first[None, :] + projected[:inner] * first_inv[:, None] + jnp.einsum('mk,mkd->md', first_mix, projected[first_neighbours])
    hidden = jax.nn.relu(pre_act).astype(jnp.bfloat16)
    second_inv = 1.0 / second_counts.astype(jnp.float32)
    second_mix = jnp.where(columns[None, :] < second_counts[:, None], second_inv[:, None], 0.0).astype(jnp.float32)
    neigh_mean = jnp.einsum('tk,tkd->td', second_mix, hidden[second_neighbours].astype(jnp.float32)).astype(jnp.bfloat16)
    logits = jnp.dot(hidden[:target], self_weight, preferred_element_type=jnp.float32) + jnp.dot(neigh_mean, neigh_weight, preferred_element_type=jnp.float32)
    probs = jax.nn.softmax(logits, axis=-1)
    onehot = (labels[:, None] == jnp.arange(classes, dtype=jnp.int32)[None, :]).astype(jnp.float32)
    dlogit = ((probs - onehot) * scale).astype(jnp.bfloat16)
    contract_rows = (((0,), (0,)), ((), ()))
    contract_cols = (((1,), (1,)), ((), ()))
    grad_self = lax.dot_general(hidden[:target], dlogit, contract_rows, preferred_element_type=jnp.float32)
    grad_neigh = lax.dot_general(neigh_mean, dlogit, contract_rows, preferred_element_type=jnp.float32)
    back_self = lax.dot_general(dlogit, self_weight, contract_cols, preferred_element_type=jnp.float32)
    back_mean = lax.dot_general(dlogit, neigh_weight, contract_cols, preferred_element_type=jnp.float32)
    grad_hidden = jnp.zeros((inner, projected.shape[1]), jnp.float32).at[:target].add(back_self)
    grad_hidden = grad_hidden.at[second_neighbours].add(second_mix[:, :, None] * back_mean[:, None, :])
    grad_pre = jnp.where(pre_act > 0, grad_hidden, 0.0).astype(jnp.float32)
    grad_bias = lax.optimization_barrier(jnp.sum(grad_pre, axis=0))
    grad_projected = jnp.zeros(projected.shape, jnp.float32).at[:inner].add(grad_pre * first_inv[:, None])
    grad_projected = grad_projected.at[first_neighbours].add(first_mix[:, :, None] * grad_pre[:, None, :])
    return (grad_projected.astype(jnp.bfloat16), grad_self, grad_neigh, grad_bias)

def reference(features, proj_weight, bias_first, self_weight, neigh_weight, first_neighbours, first_counts, second_neighbours, second_counts, labels):
    blocks = N_DP * N_MP
    scale = 1.0 / math.sqrt(MB * TGT * blocks)
    feature_blocks = features.reshape(MB * blocks, LOC, F)
    first_idx = first_neighbours.reshape(MB * blocks, MID, FAN)
    first_cnt = first_counts.reshape(MB * blocks, MID)
    second_idx = second_neighbours.reshape(MB * blocks, TGT, FAN)
    second_cnt = second_counts.reshape(MB * blocks, TGT)
    label_blocks = labels.reshape(MB * blocks, TGT)

    def step(carry, item):
        block, idx_a, cnt_a, idx_b, cnt_b, label_row = item
        projected = jnp.dot(block, proj_weight, preferred_element_type=jnp.float32)
        grads = sage_block(projected, bias_first, self_weight, neigh_weight, idx_a, cnt_a, idx_b, cnt_b, label_row, scale)
        weight_term = lax.dot_general(block, grads[0], (((0,), (0,)), ((), ())), preferred_element_type=jnp.float32)
        return ((carry[0] + weight_term, carry[1] + grads[1], carry[2] + grads[2], carry[3] + grads[3]), None)
    start = (jnp.zeros((F, D), jnp.float32), jnp.zeros((D, CLS), jnp.float32), jnp.zeros((D, CLS), jnp.float32), jnp.zeros((D,), jnp.float32))
    totals, unused = lax.scan(step, start, (feature_blocks, first_idx, first_cnt, second_idx, second_cnt, label_blocks))
    return (totals[0], totals[1], totals[2], totals[3])
```

```python
import functools
import itertools
import math

import jax
import jax.numpy as jnp
from jax import lax
from jax.experimental import pallas as pl
from jax.experimental.pallas import tpu as pltpu
from jax.sharding import PartitionSpec as P

MESH = pl.DeviceIdType.MESH
LANES = 128
TILE = 16
F32 = jnp.float32
BF16 = jnp.bfloat16
ROWS0 = (((0,), (0,)), ((), ()))
COLS1 = (((1,), (1,)), ((), ()))


def round_up(n, m):
    return (n + m - 1) // m * m


def factors_of(n):
    out = []
    for first in (2, 2):
        if n % first == 0:
            out.append(first)
            n //= first
    while n > 1:
        for f in (4, 3, 2, n):
            if n % f == 0:
                out.append(f)
                n //= f
                break
    return out


def plan_of(fs, width):
    plan = [("row", fs[0], width)]
    w = width
    for f in fs[1:]:
        if w % (f * LANES) == 0:
            w //= f
            plan.append(("col", f, w))
        else:
            plan.append(("all", f, w))
    return plan


def column(row):
    n = row.shape[1]
    r = lax.broadcasted_iota(jnp.int32, (n, n), 0)
    c = lax.broadcasted_iota(jnp.int32, (n, n), 1)
    return jnp.sum(jnp.where(r == c, row.astype(F32), 0.0), axis=1, keepdims=True)


def counts_matrix(neighbours, counts, width, start):
    fan, rows = neighbours.shape
    place = lax.broadcasted_iota(jnp.int32, (width, rows), 0)
    total = start
    for k in range(fan):
        index = jnp.where(counts > k, neighbours[k : k + 1, :], -1)
        total = total + jnp.where(index == place, 1.0, 0.0)
    return total.T


def split(x):
    high = x.astype(BF16)
    return high, (x - high.astype(F32)).astype(BF16)


def kernel(
    cfg,
    x_ref, w_ref, bias_ref, sw_ref, nw_ref, fn_ref, fc_ref, sn_ref, sc_ref, lab_ref,
    g_out, s_out,
    n1, zb, p_own, p_send, p_recv, gq, dl_s, hid_s, nm_s, part_g, part_s, cur_s, r_s,
    *rest,
):
    n_mp, n_dp, scale, fs, plan, chunks = cfg
    fan, batches, mid = fn_ref.shape
    tgt = sn_ref.shape[2]
    loc = x_ref.shape[1] // n_mp
    width = w_ref.shape[1]
    classes = sw_ref.shape[0]
    cpad = round_up(classes + 1, TILE)
    stot = s_out.shape[0]
    n_st = len(fs)
    per = 2 * n_st
    bufs = rest[: per * len(chunks)]
    (n1_ss, n1_rs, p_ss, p_rs, q_ss, q_rs, y_ss, y_rs, ya_ss, ya_rs,
     st_ss, st_rs, ag_ss, ag_rs) = rest[per * len(chunks):]

    d = lax.axis_index("dp")
    m = lax.axis_index("mp")
    mp_peer = [None] + [lax.rem(m + o, n_mp) for o in range(1, n_mp)]
    stride = [1]
    for f in fs:
        stride.append(stride[-1] * f)
    digit = [lax.rem(d // stride[k], fs[k]) for k in range(n_st)]

    def dp_peer(k, o):
        other = lax.rem(digit[k] + o, fs[k])
        return other, (d + (other - digit[k]) * stride[k], m)

    partners = [(d, mp_peer[o]) for o in range(1, n_mp)]
    for k in range(n_st):
        partners += [dp_peer(k, o)[1] for o in range(1, fs[k])]

    barrier = pltpu.get_barrier_semaphore()
    for who in partners:
        pl.semaphore_signal(barrier, inc=1, device_id=who, device_id_type=MESH)

    def remote(src, dst, ss, rs, who):
        return pltpu.make_async_remote_copy(
            src_ref=src, dst_ref=dst, send_sem=ss, recv_sem=rs, device_id=who, device_id_type=MESH
        )

    sends = []

    inv1 = []
    for i in range(batches):
        cnt = column(fc_ref[i : i + 1, :])
        inv1.append(1.0 / (cnt + 1.0))
        r = lax.broadcasted_iota(jnp.int32, (loc, mid), 0)
        c = lax.broadcasted_iota(jnp.int32, (loc, mid), 1)
        eye = jnp.where(r == c, 1.0, 0.0)
        n1[m, i * mid : (i + 1) * mid, :] = counts_matrix(fn_ref[:, i, :], fc_ref[i : i + 1, :], loc, eye).astype(BF16)
    pl.semaphore_wait(barrier, len(partners))
    n1_copies = []
    for o in range(1, n_mp):
        cp = remote(n1.at[m], n1.at[m], n1_ss.at[o], n1_rs.at[o], (d, mp_peer[o]))
        cp.start()
        n1_copies.append(cp)

    def project(q):
        rows = pl.ds(pl.multiple_of(q * loc, loc), loc)
        zs = []
        for i in range(batches):
            zs.append(jnp.dot(n1[q, i * mid : (i + 1) * mid, :], x_ref[i, rows, :],
                              preferred_element_type=F32))
        z = jnp.concatenate(zs, axis=0)
        high, low = split(z)
        zb[:, pl.ds(pl.multiple_of(q * batches * mid, LANES), batches * mid)] = z.T.astype(BF16)
        return (jnp.dot(high, w_ref[...], preferred_element_type=F32)
                + jnp.dot(low, w_ref[...], preferred_element_type=F32))

    p_own[...] = project(m)
    p_copies = {}
    for o in range(1, n_mp):
        n1_copies[o - 1].wait_recv()
    for o in range(1, n_mp):
        p_send[o - 1] = project(mp_peer[o])
        for i in range(batches):
            rows = slice(i * mid, (i + 1) * mid)
            cp = remote(p_send.at[o - 1, rows], p_recv.at[o - 1, rows],
                        p_ss.at[o, i], p_rs.at[o, i], (d, mp_peer[o]))
            cp.start()
            p_copies[o, i] = cp

    inv2, mix, n2s, hot = [], [], [], []
    for i in range(batches):
        cnt = column(sc_ref[i : i + 1, :])
        inv2.append(1.0 / cnt)
        n2 = counts_matrix(sn_ref[:, i, :], sc_ref[i : i + 1, :], mid, jnp.zeros((mid, tgt), F32))
        n2s.append(n2.astype(BF16))
        r = lax.broadcasted_iota(jnp.int32, (tgt, mid), 0)
        c = lax.broadcasted_iota(jnp.int32, (tgt, mid), 1)
        both = jnp.concatenate([jnp.where(r == c, 1.0, 0.0), n2], axis=0)
        mix.append(jnp.concatenate([both, both], axis=0).astype(BF16))
        lab = column(lab_ref[i : i + 1, :])
        lane = lax.broadcasted_iota(jnp.int32, (tgt, classes), 1).astype(F32)
        hot.append(jnp.where(lane == lab, 1.0, 0.0))
    dl_s[...] = jnp.zeros(dl_s.shape, F32)

    q_copies = {}
    bias_sum = jnp.zeros((1, width), F32)
    for i in range(batches):
        rows = slice(i * mid, (i + 1) * mid)
        total = p_own[rows, :]
        for o in range(1, n_mp):
            p_copies[o, i].wait_recv()
            total = total + p_recv[o - 1, rows, :]
        pre = bias_ref[...] + total * inv1[i]
        hidden = jnp.maximum(pre, 0.0).astype(BF16)
        top = hidden[:tgt]
        mean = (jnp.dot(n2s[i], hidden, preferred_element_type=F32) * inv2[i]).astype(BF16)
        logits = (lax.dot_general(top, sw_ref[...], COLS1, preferred_element_type=F32)
                  + lax.dot_general(mean, nw_ref[...], COLS1, preferred_element_type=F32))
        e = jnp.exp(logits - jnp.max(logits, axis=1, keepdims=True))
        probs = e / jnp.sum(e, axis=1, keepdims=True)
        dl = (probs - hot[i]) * scale
        here = slice(i * tgt, (i + 1) * tgt)
        dl_s[here, :classes] = dl
        hid_s[here, :] = top
        nm_s[here, :] = mean
        dlb = dl.astype(BF16)
        back_self = jnp.dot(dlb, sw_ref[...], preferred_element_type=F32)
        back_mean = jnp.dot(dlb, nw_ref[...], preferred_element_type=F32) * inv2[i]
        high, low = split(jnp.concatenate([back_self, back_mean], axis=0))
        grad_hidden = lax.dot_general(mix[i], jnp.concatenate([high, low], axis=0), ROWS0,
                                      preferred_element_type=F32)
        grad_pre = jnp.where(pre > 0, grad_hidden, 0.0)
        bias_sum = bias_sum + jnp.sum(grad_pre, axis=0, keepdims=True)
        gq[m, rows, :] = (grad_pre * inv1[i]).astype(BF16)
        for o in range(1, n_mp):
            cp = remote(gq.at[m, rows], gq.at[m, rows], q_ss.at[o, i], q_rs.at[o, i],
                        (d, mp_peer[o]))
            cp.start()
            q_copies[o, i] = cp

    dlb = dl_s[...].astype(BF16)
    own = lax.dot_general(dlb, hid_s[...], ROWS0, preferred_element_type=F32)
    neigh = lax.dot_general(dlb, nm_s[...], ROWS0, preferred_element_type=F32)
    row = lax.broadcasted_iota(jnp.int32, own.shape, 0)
    own = jnp.where(row == classes, bias_sum, own)
    srows = stot // n_mp
    everything = [own, neigh]
    if stot > 2 * cpad:
        everything.append(jnp.zeros((stot - 2 * cpad, width), F32))
    part_s[...] = jnp.concatenate(everything, axis=0).astype(BF16).reshape(n_mp, srows, width)

    def chain(ci, part, prefix):
        ag = bufs[ci * per + per - 1]
        cur = part
        for k, (kind, f, w) in enumerate(plan):
            recv = bufs[ci * per + 2 * k]
            copies = []
            for o in range(1, f):
                other, who = dp_peer(k, o)
                if kind == "all":
                    src, dst = cur, recv.at[digit[k]]
                else:
                    src, dst = cur.at[other], recv.at[o - 1]
                cp = remote(src, dst, st_ss.at[ci, k, o], st_rs.at[ci, k, o], who)
                cp.start()
                copies.append(cp)
            if kind == "all":
                recv[digit[k]] = cur[...]
            sends.extend(copies)
            yield
            for cp in copies:
                cp.wait_recv()
            if kind == "all":
                acc = recv[0].astype(F32)
                for j in range(1, f):
                    acc = acc + recv[j].astype(F32)
            else:
                acc = cur[digit[k]].astype(F32)
                for o in range(1, f):
                    acc = acc + recv[o - 1].astype(F32)
                prefix = prefix + (digit[k],)
            acc = acc.astype(BF16)
            if k == n_st - 1:
                ag[prefix] = acc
            else:
                nxt = bufs[ci * per + 2 * k + 1]
                if plan[k + 1][0] == "col":
                    step = plan[k + 1][2]
                    for j in range(plan[k + 1][1]):
                        nxt[j] = acc[:, j * step : (j + 1) * step]
                else:
                    nxt[...] = acc
                cur = nxt
        for k in reversed(range(n_st)):
            kind, f, w = plan[k]
            if kind == "all":
                continue
            copies = []
            for o in range(1, f):
                cp = remote(ag.at[prefix], ag.at[prefix], ag_ss.at[ci, k, o], ag_rs.at[ci, k, o],
                            dp_peer(k, o)[1])
                cp.start()
                copies.append(cp)
            sends.extend(copies)
            prefix = prefix[:-1]
            yield
            for cp in copies:
                cp.wait_recv()

    def spread(ag, lead, out, row0):
        parts = ag.shape[len(lead) : -2]
        half, w = ag.shape[-2:]
        for at in itertools.product(*[range(f) for f in parts]):
            col = 0
            for f, j in zip(parts[1:], at[1:]):
                col = col * f + j
            out[row0 + at[0] * half : row0 + (at[0] + 1) * half, col * w : (col + 1) * w] = (
                ag[lead + at])

    def s_chain():
        copies = []
        for o in range(1, n_mp):
            cp = remote(part_s.at[mp_peer[o]], r_s.at[o - 1], y_ss.at[o], y_rs.at[o],
                        (d, mp_peer[o]))
            cp.start()
            copies.append(cp)
        sends.extend(copies)
        yield
        for cp in copies:
            cp.wait_recv()
        acc = part_s[m].astype(F32)
        for o in range(1, n_mp):
            acc = acc + r_s[o - 1].astype(F32)
        cur_s[...] = acc.astype(BF16).reshape(cur_s.shape)
        yield from chain(0, cur_s, (m,))
        ag = bufs[per - 1]
        copies = []
        for o in range(1, n_mp):
            cp = remote(ag.at[m], ag.at[m], ya_ss.at[o], ya_rs.at[o], (d, mp_peer[o]))
            cp.start()
            copies.append(cp)
        sends.extend(copies)
        yield
        for cp in copies:
            cp.wait_recv()
        for q in range(n_mp):
            spread(ag, (q,), s_out, q * srows)

    def g_chain(ci, row0):
        rows = chunks[ci]
        part = part_g.at[ci - 1]
        part[...] = jnp.dot(
            zb[row0 : row0 + rows, :], gall, preferred_element_type=F32
        ).astype(BF16).reshape(part.shape)
        yield from chain(ci, part, ())
        spread(bufs[ci * per + per - 1], (), g_out, row0)

    live = [s_chain()]
    next(live[0])
    for cp in q_copies.values():
        cp.wait_recv()
    gall = gq[...].reshape(n_mp * batches * mid, width)
    row0 = 0
    for ci in range(1, len(chunks)):
        gen = g_chain(ci, row0)
        next(gen)
        live.append(gen)
        row0 += chunks[ci]
    while live:
        for gen in list(live):
            try:
                next(gen)
            except StopIteration:
                live.remove(gen)

    for cp in n1_copies + list(p_copies.values()) + list(q_copies.values()) + sends:
        cp.wait_send()


def local(
    n_dp, n_mp,
    features, proj_weight, bias_first, self_weight, neigh_weight,
    first_neighbours, first_counts, second_neighbours, second_counts, labels,
):
    batches, _, depth = features.shape
    width = proj_weight.shape[1]
    mid = first_neighbours.shape[1]
    loc = features.shape[1] // n_mp
    tgt = labels.shape[1]
    classes = self_weight.shape[1]
    scale = 1.0 / math.sqrt(batches * tgt * n_dp * n_mp)
    fs = factors_of(n_dp)
    cpad = round_up(classes + 1, TILE)
    stot = round_up(2 * cpad, TILE * fs[0] * n_mp)
    parts = 3
    chunks = [stot // n_mp] + [depth // parts] * parts
    n_st = len(fs)

    plan = plan_of(fs, width)
    bufs = []
    for ci, rows in enumerate(chunks):
        half = rows // fs[0]
        for k, (kind, f, w) in enumerate(plan):
            bufs.append(pltpu.VMEM((f if kind == "all" else f - 1, half, w), BF16))
            if k < n_st - 1 and plan[k + 1][0] == "col":
                bufs.append(pltpu.VMEM((plan[k + 1][1], half, plan[k + 1][2]), BF16))
            elif k < n_st - 1:
                bufs.append(pltpu.VMEM((half, w), BF16))
            else:
                lead = tuple(f for kind, f, w in plan if kind != "all")
                lead = ((n_mp,) if ci == 0 else ()) + lead
                bufs.append(pltpu.VMEM((*lead, half, w), BF16))
    peers = n_mp - 1
    most = max(fs)
    dma = pltpu.SemaphoreType.DMA
    stage = (len(chunks), n_st, most)
    scratch = [
        pltpu.VMEM((n_mp, batches * mid, loc), BF16),
        pltpu.VMEM((depth, n_mp * batches * mid), BF16),
        pltpu.VMEM((batches * mid, width), F32),
        pltpu.VMEM((peers, batches * mid, width), F32),
        pltpu.VMEM((peers, batches * mid, width), F32),
        pltpu.VMEM((n_mp, batches * mid, width), BF16),
        pltpu.VMEM((batches * tgt, cpad), F32),
        pltpu.VMEM((batches * tgt, width), BF16),
        pltpu.VMEM((batches * tgt, width), BF16),
        pltpu.VMEM((parts, fs[0], depth // parts // fs[0], width), BF16),
        pltpu.VMEM((n_mp, stot // n_mp, width), BF16),
        pltpu.VMEM((fs[0], stot // n_mp // fs[0], width), BF16),
        pltpu.VMEM((peers, stot // n_mp, width), BF16),
        *bufs,
        dma((n_mp,)), dma((n_mp,)),
        dma((n_mp, batches)), dma((n_mp, batches)),
        dma((n_mp, batches)), dma((n_mp, batches)),
        dma((n_mp,)), dma((n_mp,)),
        dma((n_mp,)), dma((n_mp,)),
        dma(stage), dma(stage), dma(stage), dma(stage),
    ]
    vmem = pl.BlockSpec(memory_space=pltpu.VMEM)
    g, s = pl.pallas_call(
        functools.partial(kernel, (n_mp, n_dp, scale, fs, plan, chunks)),
        out_shape=(
            jax.ShapeDtypeStruct((depth, width), BF16),
            jax.ShapeDtypeStruct((stot, width), BF16),
        ),
        in_specs=[vmem] * 10,
        out_specs=(vmem, vmem),
        scratch_shapes=scratch,
        compiler_params=pltpu.CompilerParams(
            collective_id=0, has_side_effects=True, vmem_limit_bytes=40 * 1024 * 1024
        ),
    )(
        features, proj_weight, bias_first.reshape(1, width), self_weight.T, neigh_weight.T,
        first_neighbours.transpose(2, 0, 1), first_counts,
        second_neighbours.transpose(2, 0, 1), second_counts, labels,
    )
    return (
        g.astype(F32),
        s[:classes].T.astype(F32),
        s[cpad : cpad + classes].T.astype(F32),
        s[classes].astype(F32),
    )


def solution(mesh):
    placed = (
        P(None, "dp", "mp"),
        P("mp", None),
        P(),
        P(),
        P(),
        P(None, ("dp", "mp"), None),
        P(None, ("dp", "mp")),
        P(None, ("dp", "mp"), None),
        P(None, ("dp", "mp")),
        P(None, ("dp", "mp")),
    )
    body = functools.partial(local, mesh.shape["dp"], mesh.shape["mp"])
    return jax.shard_map(
        body, mesh=mesh, in_specs=placed, out_specs=(P("mp", None), P(), P(), P()), check_vma=False
    )
```

```python
import functools
import itertools
import math

import jax
import jax.numpy as jnp
from jax import lax
from jax.experimental import pallas as pl
from jax.experimental.pallas import tpu as pltpu
from jax.sharding import PartitionSpec as P

MESH = pl.DeviceIdType.MESH
LANES = 128
TILE = 16
F32 = jnp.float32
BF16 = jnp.bfloat16
ROWS0 = (((0,), (0,)), ((), ()))
COLS1 = (((1,), (1,)), ((), ()))


def round_up(n, m):
    return (n + m - 1) // m * m


def factors_of(n):
    out = []
    for first in (2, 2):
        if n % first == 0:
            out.append(first)
            n //= first
    while n > 1:
        for f in (4, 3, 2, n):
            if n % f == 0:
                out.append(f)
                n //= f
                break
    return out


def plan_of(fs, width, shards):
    plan = [(0, "row", fs[0], width)]
    if shards > 1:
        plan.append((len(fs), "row", shards, width))
    w = width
    for axis, f in list(enumerate(fs))[1:]:
        if w % (f * LANES) == 0:
            w //= f
            plan.append((axis, "col", f, w))
        else:
            plan.append((axis, "all", f, w))
    return plan


def column(row):
    n = row.shape[1]
    r = lax.broadcasted_iota(jnp.int32, (n, n), 0)
    c = lax.broadcasted_iota(jnp.int32, (n, n), 1)
    return jnp.sum(jnp.where(r == c, row.astype(F32), 0.0), axis=1, keepdims=True)


def counts_matrix(neighbours, counts, width, start):
    fan, rows = neighbours.shape
    place = lax.broadcasted_iota(jnp.int32, (width, rows), 0)
    total = start
    for k in range(fan):
        index = jnp.where(counts > k, neighbours[k : k + 1, :], -1)
        total = total + jnp.where(index == place, 1.0, 0.0)
    return total.T


def split(x):
    high = x.astype(BF16)
    return high, (x - high.astype(F32)).astype(BF16)


def kernel(
    cfg,
    x_ref, w_ref, bias_ref, sw_ref, nw_ref, fn_ref, fc_ref, sn_ref, sc_ref, lab_ref,
    g_out, s_out,
    n1, zb, p_own, p_send, p_recv, gq, dl_s, hid_s, nm_s, part_g, part_s,
    *rest,
):
    n_mp, n_dp, scale, fs, plans, chunks = cfg
    fan, batches, mid = fn_ref.shape
    tgt = sn_ref.shape[2]
    loc = x_ref.shape[1] // n_mp
    width = w_ref.shape[1]
    classes = sw_ref.shape[0]
    cpad = round_up(classes + 1, TILE)
    stot = s_out.shape[0]
    n_st = len(fs)
    bases = [0]
    for plan in plans:
        bases.append(bases[-1] + 2 * len(plan))
    bufs = rest[: bases[-1]]
    (n1_ss, n1_rs, p_ss, p_rs, q_ss, q_rs,
     st_ss, st_rs, ag_ss, ag_rs) = rest[bases[-1]:]

    d = lax.axis_index("dp")
    m = lax.axis_index("mp")
    mp_peer = [None] + [lax.rem(m + o, n_mp) for o in range(1, n_mp)]
    stride = [1]
    for f in fs:
        stride.append(stride[-1] * f)
    digit = [lax.rem(d // stride[k], fs[k]) for k in range(n_st)]

    digit.append(m)

    def dp_peer(k, o):
        if k == n_st:
            return mp_peer[o], (d, mp_peer[o])
        other = lax.rem(digit[k] + o, fs[k])
        return other, (d + (other - digit[k]) * stride[k], m)

    partners = [(d, mp_peer[o]) for o in range(1, n_mp)]
    for k in range(n_st):
        partners += [dp_peer(k, o)[1] for o in range(1, fs[k])]

    barrier = pltpu.get_barrier_semaphore()
    for who in partners:
        pl.semaphore_signal(barrier, inc=1, device_id=who, device_id_type=MESH)

    def remote(src, dst, ss, rs, who):
        return pltpu.make_async_remote_copy(
            src_ref=src, dst_ref=dst, send_sem=ss, recv_sem=rs, device_id=who, device_id_type=MESH
        )

    sends = []

    inv1 = []
    for i in range(batches):
        cnt = column(fc_ref[i : i + 1, :])
        inv1.append(1.0 / (cnt + 1.0))
        r = lax.broadcasted_iota(jnp.int32, (loc, mid), 0)
        c = lax.broadcasted_iota(jnp.int32, (loc, mid), 1)
        eye = jnp.where(r == c, 1.0, 0.0)
        n1[m, i * mid : (i + 1) * mid, :] = counts_matrix(fn_ref[:, i, :], fc_ref[i : i + 1, :], loc, eye).astype(BF16)
    pl.semaphore_wait(barrier, len(partners))
    n1_copies = []
    for o in range(1, n_mp):
        cp = remote(n1.at[m], n1.at[m], n1_ss.at[o], n1_rs.at[o], (d, mp_peer[o]))
        cp.start()
        n1_copies.append(cp)

    def project(q):
        rows = pl.ds(pl.multiple_of(q * loc, loc), loc)
        zs = []
        for i in range(batches):
            zs.append(jnp.dot(n1[q, i * mid : (i + 1) * mid, :], x_ref[i, rows, :],
                              preferred_element_type=F32))
        z = jnp.concatenate(zs, axis=0)
        high, low = split(z)
        zb[:, pl.ds(pl.multiple_of(q * batches * mid, LANES), batches * mid)] = z.T.astype(BF16)
        return (jnp.dot(high, w_ref[...], preferred_element_type=F32)
                + jnp.dot(low, w_ref[...], preferred_element_type=F32))

    p_own[...] = project(m)
    p_copies = {}
    for o in range(1, n_mp):
        n1_copies[o - 1].wait_recv()
    for o in range(1, n_mp):
        p_send[o - 1] = project(mp_peer[o])
        for i in range(batches):
            rows = slice(i * mid, (i + 1) * mid)
            cp = remote(p_send.at[o - 1, rows], p_recv.at[o - 1, rows],
                        p_ss.at[o, i], p_rs.at[o, i], (d, mp_peer[o]))
            cp.start()
            p_copies[o, i] = cp

    inv2, mix, n2s, hot = [], [], [], []
    for i in range(batches):
        cnt = column(sc_ref[i : i + 1, :])
        inv2.append(1.0 / cnt)
        n2 = counts_matrix(sn_ref[:, i, :], sc_ref[i : i + 1, :], mid, jnp.zeros((mid, tgt), F32))
        n2s.append(n2.astype(BF16))
        r = lax.broadcasted_iota(jnp.int32, (tgt, mid), 0)
        c = lax.broadcasted_iota(jnp.int32, (tgt, mid), 1)
        both = jnp.concatenate([jnp.where(r == c, 1.0, 0.0), n2], axis=0)
        mix.append(jnp.concatenate([both, both], axis=0).astype(BF16))
        lab = column(lab_ref[i : i + 1, :])
        lane = lax.broadcasted_iota(jnp.int32, (tgt, classes), 1).astype(F32)
        hot.append(jnp.where(lane == lab, 1.0, 0.0))
    dl_s[...] = jnp.zeros(dl_s.shape, F32)

    q_copies = {}
    bias_sum = jnp.zeros((1, width), F32)
    for i in range(batches):
        rows = slice(i * mid, (i + 1) * mid)
        total = p_own[rows, :]
        for o in range(1, n_mp):
            p_copies[o, i].wait_recv()
            total = total + p_recv[o - 1, rows, :]
        pre = bias_ref[...] + total * inv1[i]
        hidden = jnp.maximum(pre, 0.0).astype(BF16)
        top = hidden[:tgt]
        mean = (jnp.dot(n2s[i], hidden, preferred_element_type=F32) * inv2[i]).astype(BF16)
        logits = (lax.dot_general(top, sw_ref[...], COLS1, preferred_element_type=F32)
                  + lax.dot_general(mean, nw_ref[...], COLS1, preferred_element_type=F32))
        e = jnp.exp(logits - jnp.max(logits, axis=1, keepdims=True))
        probs = e / jnp.sum(e, axis=1, keepdims=True)
        dl = (probs - hot[i]) * scale
        here = slice(i * tgt, (i + 1) * tgt)
        dl_s[here, :classes] = dl
        hid_s[here, :] = top
        nm_s[here, :] = mean
        dlb = dl.astype(BF16)
        back_self = jnp.dot(dlb, sw_ref[...], preferred_element_type=F32)
        back_mean = jnp.dot(dlb, nw_ref[...], preferred_element_type=F32) * inv2[i]
        high, low = split(jnp.concatenate([back_self, back_mean], axis=0))
        grad_hidden = lax.dot_general(mix[i], jnp.concatenate([high, low], axis=0), ROWS0,
                                      preferred_element_type=F32)
        grad_pre = jnp.where(pre > 0, grad_hidden, 0.0)
        bias_sum = bias_sum + jnp.sum(grad_pre, axis=0, keepdims=True)
        gq[m, rows, :] = (grad_pre * inv1[i]).astype(BF16)
        for o in range(1, n_mp):
            cp = remote(gq.at[m, rows], gq.at[m, rows], q_ss.at[o, i], q_rs.at[o, i],
                        (d, mp_peer[o]))
            cp.start()
            q_copies[o, i] = cp

    dlb = dl_s[...].astype(BF16)
    own = lax.dot_general(dlb, hid_s[...], ROWS0, preferred_element_type=F32)
    neigh = lax.dot_general(dlb, nm_s[...], ROWS0, preferred_element_type=F32)
    row = lax.broadcasted_iota(jnp.int32, own.shape, 0)
    own = jnp.where(row == classes, bias_sum, own)
    everything = [own, neigh]
    if stot > 2 * cpad:
        everything.append(jnp.zeros((stot - 2 * cpad, width), F32))
    part_s[...] = jnp.concatenate(everything, axis=0).astype(BF16).reshape(part_s.shape)

    def chain(ci, part, prefix):
        plan, base = plans[ci], bases[ci]
        ag = bufs[bases[ci + 1] - 1]
        cur = part
        for at, (k, kind, f, w) in enumerate(plan):
            recv = bufs[base + 2 * at]
            copies = []
            for o in range(1, f):
                other, who = dp_peer(k, o)
                if kind == "all":
                    src, dst = cur, recv.at[digit[k]]
                else:
                    src, dst = cur.at[other], recv.at[o - 1]
                cp = remote(src, dst, st_ss.at[ci, k, o], st_rs.at[ci, k, o], who)
                cp.start()
                copies.append(cp)
            if kind == "all":
                recv[digit[k]] = cur[...]
            sends.extend(copies)
            yield
            for cp in copies:
                cp.wait_recv()
            if kind == "all":
                acc = recv[0].astype(F32)
                for j in range(1, f):
                    acc = acc + recv[j].astype(F32)
            else:
                acc = cur[digit[k]].astype(F32)
                for o in range(1, f):
                    acc = acc + recv[o - 1].astype(F32)
                prefix = prefix + (digit[k],)
            acc = acc.astype(BF16)
            if at == len(plan) - 1:
                ag[prefix] = acc
            else:
                nxt = bufs[base + 2 * at + 1]
                following = plan[at + 1]
                if following[1] == "col":
                    step = following[3]
                    for j in range(following[2]):
                        nxt[j] = acc[:, j * step : (j + 1) * step]
                else:
                    nxt[...] = acc.reshape(nxt.shape)
                cur = nxt
        for k, kind, f, w in reversed(plan):
            if kind == "all":
                continue
            copies = []
            for o in range(1, f):
                cp = remote(ag.at[prefix], ag.at[prefix], ag_ss.at[ci, k, o], ag_rs.at[ci, k, o],
                            dp_peer(k, o)[1])
                cp.start()
                copies.append(cp)
            sends.extend(copies)
            prefix = prefix[:-1]
            yield
            for cp in copies:
                cp.wait_recv()

    def spread(ci, out, row0):
        ag = bufs[bases[ci + 1] - 1]
        kept = [(kind, f) for k, kind, f, w in plans[ci] if kind != "all"]
        half, w = ag.shape[-2:]
        for at in itertools.product(*[range(f) for kind, f in kept]):
            row = col = 0
            for (kind, f), j in zip(kept, at):
                if kind == "row":
                    row = row * f + j
                else:
                    col = col * f + j
            top = row0 + row * half
            out[top : top + half, col * w : (col + 1) * w] = ag[at]

    def s_chain():
        yield from chain(0, part_s, ())
        spread(0, s_out, 0)

    def g_chain(ci, row0):
        rows = chunks[ci]
        part = part_g.at[ci - 1]
        part[...] = jnp.dot(
            zb[row0 : row0 + rows, :], gall, preferred_element_type=F32
        ).astype(BF16).reshape(part.shape)
        yield from chain(ci, part, ())
        spread(ci, g_out, row0)

    live = [s_chain()]
    next(live[0])
    for cp in q_copies.values():
        cp.wait_recv()
    gall = gq[...].reshape(n_mp * batches * mid, width)
    row0 = 0
    for ci in range(1, len(chunks)):
        gen = g_chain(ci, row0)
        next(gen)
        live.append(gen)
        row0 += chunks[ci]
    while live:
        for gen in list(live):
            try:
                next(gen)
            except StopIteration:
                live.remove(gen)

    for cp in n1_copies + list(p_copies.values()) + list(q_copies.values()) + sends:
        cp.wait_send()


def local(
    n_dp, n_mp,
    features, proj_weight, bias_first, self_weight, neigh_weight,
    first_neighbours, first_counts, second_neighbours, second_counts, labels,
):
    batches, _, depth = features.shape
    width = proj_weight.shape[1]
    mid = first_neighbours.shape[1]
    loc = features.shape[1] // n_mp
    tgt = labels.shape[1]
    classes = self_weight.shape[1]
    scale = 1.0 / math.sqrt(batches * tgt * n_dp * n_mp)
    fs = factors_of(n_dp)
    cpad = round_up(classes + 1, TILE)
    stot = round_up(2 * cpad, TILE * fs[0] * n_mp)
    parts = 3
    chunks = [stot] + [depth // parts] * parts
    n_st = len(fs)

    plans = [plan_of(fs, width, n_mp)] + [plan_of(fs, width, 1)] * parts
    bufs = []
    for plan, rows in zip(plans, chunks):
        for at, (k, kind, f, w) in enumerate(plan):
            if kind == "row":
                rows //= f
            bufs.append(pltpu.VMEM((f if kind == "all" else f - 1, rows, w), BF16))
            if at == len(plan) - 1:
                lead = tuple(f for k, kind, f, w in plan if kind != "all")
                bufs.append(pltpu.VMEM((*lead, rows, w), BF16))
            else:
                _, then, g, left = plan[at + 1]
                if then == "row":
                    bufs.append(pltpu.VMEM((g, rows // g, left), BF16))
                elif then == "col":
                    bufs.append(pltpu.VMEM((g, rows, left), BF16))
                else:
                    bufs.append(pltpu.VMEM((rows, left), BF16))
    peers = n_mp - 1
    most = max(*fs, n_mp)
    dma = pltpu.SemaphoreType.DMA
    stage = (len(chunks), n_st + 1, most)
    scratch = [
        pltpu.VMEM((n_mp, batches * mid, loc), BF16),
        pltpu.VMEM((depth, n_mp * batches * mid), BF16),
        pltpu.VMEM((batches * mid, width), F32),
        pltpu.VMEM((peers, batches * mid, width), F32),
        pltpu.VMEM((peers, batches * mid, width), F32),
        pltpu.VMEM((n_mp, batches * mid, width), BF16),
        pltpu.VMEM((batches * tgt, cpad), F32),
        pltpu.VMEM((batches * tgt, width), BF16),
        pltpu.VMEM((batches * tgt, width), BF16),
        pltpu.VMEM((parts, fs[0], depth // parts // fs[0], width), BF16),
        pltpu.VMEM((fs[0], stot // fs[0], width), BF16),
        *bufs,
        dma((n_mp,)), dma((n_mp,)),
        dma((n_mp, batches)), dma((n_mp, batches)),
        dma((n_mp, batches)), dma((n_mp, batches)),
        dma(stage), dma(stage), dma(stage), dma(stage),
    ]
    vmem = pl.BlockSpec(memory_space=pltpu.VMEM)
    g, s = pl.pallas_call(
        functools.partial(kernel, (n_mp, n_dp, scale, fs, plans, chunks)),
        out_shape=(
            jax.ShapeDtypeStruct((depth, width), BF16),
            jax.ShapeDtypeStruct((stot, width), BF16),
        ),
        in_specs=[vmem] * 10,
        out_specs=(vmem, vmem),
        scratch_shapes=scratch,
        compiler_params=pltpu.CompilerParams(
            collective_id=0, has_side_effects=True, vmem_limit_bytes=40 * 1024 * 1024
        ),
    )(
        features, proj_weight, bias_first.reshape(1, width), self_weight.T, neigh_weight.T,
        first_neighbours.transpose(2, 0, 1), first_counts,
        second_neighbours.transpose(2, 0, 1), second_counts, labels,
    )
    return (
        g.astype(F32),
        s[:classes].T.astype(F32),
        s[cpad : cpad + classes].T.astype(F32),
        s[classes].astype(F32),
    )


def solution(mesh):
    placed = (
        P(None, "dp", "mp"),
        P("mp", None),
        P(),
        P(),
        P(),
        P(None, ("dp", "mp"), None),
        P(None, ("dp", "mp")),
        P(None, ("dp", "mp"), None),
        P(None, ("dp", "mp")),
        P(None, ("dp", "mp")),
    )
    body = functools.partial(local, mesh.shape["dp"], mesh.shape["mp"])
    return jax.shard_map(
        body, mesh=mesh, in_specs=placed, out_specs=(P("mp", None), P(), P(), P()), check_vma=False
    )
```

```python
import functools
import itertools
import math

import jax
import jax.numpy as jnp
from jax import lax
from jax.experimental import pallas as pl
from jax.experimental.pallas import tpu as pltpu
from jax.sharding import PartitionSpec as P

MESH = pl.DeviceIdType.MESH
LANES = 128
TILE = 16
F32 = jnp.float32
BF16 = jnp.bfloat16
ROWS0 = (((0,), (0,)), ((), ()))
COLS1 = (((1,), (1,)), ((), ()))


def round_up(n, m):
    return (n + m - 1) // m * m


def factors_of(n):
    out = []
    for first in (2, 2):
        if n % first == 0:
            out.append(first)
            n //= first
    while n > 1:
        for f in (4, 3, 2, n):
            if n % f == 0:
                out.append(f)
                n //= f
                break
    return out


def plan_of(fs, width, shards):
    plan = [(0, "row", fs[0], width)]
    if shards > 1:
        plan.append((len(fs), "row", shards, width))
    w = width
    for axis, f in list(enumerate(fs))[1:]:
        if w % (f * LANES) == 0:
            w //= f
            plan.append((axis, "col", f, w))
        else:
            plan.append((axis, "all", f, w))
    return plan


def column(row):
    n = row.shape[1]
    r = lax.broadcasted_iota(jnp.int32, (n, n), 0)
    c = lax.broadcasted_iota(jnp.int32, (n, n), 1)
    return jnp.sum(jnp.where(r == c, row.astype(F32), 0.0), axis=1, keepdims=True)


def counts_matrix(neighbours, counts, width, start):
    fan, rows = neighbours.shape
    place = lax.broadcasted_iota(jnp.int32, (width, rows), 0)
    total = start
    for k in range(fan):
        index = jnp.where(counts > k, neighbours[k : k + 1, :], -1)
        total = total + jnp.where(index == place, 1.0, 0.0)
    return total.T


def split(x):
    high = x.astype(BF16)
    return high, (x - high.astype(F32)).astype(BF16)


def kernel(
    cfg,
    x_ref, w_ref, bias_ref, sw_ref, nw_ref, ids_ref,
    g_out, s_out,
    n1, zb, p_own, p_send, p_recv, gq, dl_s, hid_s, nm_s, part_g, part_s,
    *rest,
):
    n_mp, n_dp, scale, fs, plans, chunks, tgt = cfg
    packed, batches, mid = ids_ref.shape
    fan = (packed - 3) // 2
    loc = x_ref.shape[1] // n_mp
    width = w_ref.shape[1]
    classes = sw_ref.shape[0]
    cpad = round_up(classes + 1, TILE)
    stot = s_out.shape[0]
    n_st = len(fs)
    bases = [0]
    for plan in plans:
        bases.append(bases[-1] + 2 * len(plan))
    bufs = rest[: bases[-1]]
    (n1_ss, n1_rs, p_ss, p_rs, q_ss, q_rs,
     st_ss, st_rs, ag_ss, ag_rs) = rest[bases[-1]:]

    d = lax.axis_index("dp")
    m = lax.axis_index("mp")
    mp_peer = [None] + [lax.rem(m + o, n_mp) for o in range(1, n_mp)]
    stride = [1]
    for f in fs:
        stride.append(stride[-1] * f)
    digit = [lax.rem(d // stride[k], fs[k]) for k in range(n_st)]

    digit.append(m)

    def dp_peer(k, o):
        if k == n_st:
            return mp_peer[o], (d, mp_peer[o])
        other = lax.rem(digit[k] + o, fs[k])
        return other, (d + (other - digit[k]) * stride[k], m)

    partners = [(d, mp_peer[o]) for o in range(1, n_mp)]
    for k in range(n_st):
        partners += [dp_peer(k, o)[1] for o in range(1, fs[k])]

    barrier = pltpu.get_barrier_semaphore()
    for who in partners:
        pl.semaphore_signal(barrier, inc=1, device_id=who, device_id_type=MESH)

    def remote(src, dst, ss, rs, who):
        return pltpu.make_async_remote_copy(
            src_ref=src, dst_ref=dst, send_sem=ss, recv_sem=rs, device_id=who, device_id_type=MESH
        )

    sends = []

    inv1 = []
    for i in range(batches):
        cnt = column(ids_ref[fan, i : i + 1, :])
        inv1.append(1.0 / (cnt + 1.0))
        r = lax.broadcasted_iota(jnp.int32, (loc, mid), 0)
        c = lax.broadcasted_iota(jnp.int32, (loc, mid), 1)
        eye = jnp.where(r == c, 1.0, 0.0)
        n1[m, i * mid : (i + 1) * mid, :] = counts_matrix(ids_ref[:fan, i, :], ids_ref[fan, i : i + 1, :], loc, eye).astype(BF16)
    pl.semaphore_wait(barrier, len(partners))
    n1_copies = []
    for o in range(1, n_mp):
        cp = remote(n1.at[m], n1.at[m], n1_ss.at[o], n1_rs.at[o], (d, mp_peer[o]))
        cp.start()
        n1_copies.append(cp)

    def project(q):
        rows = pl.ds(pl.multiple_of(q * loc, loc), loc)
        zs = []
        for i in range(batches):
            zs.append(jnp.dot(n1[q, i * mid : (i + 1) * mid, :], x_ref[i, rows, :],
                              preferred_element_type=F32))
        z = jnp.concatenate(zs, axis=0)
        high, low = split(z)
        zb[:, pl.ds(pl.multiple_of(q * batches * mid, LANES), batches * mid)] = z.T.astype(BF16)
        return (jnp.dot(high, w_ref[...], preferred_element_type=F32)
                + jnp.dot(low, w_ref[...], preferred_element_type=F32))

    p_own[...] = project(m)
    p_copies = {}
    for o in range(1, n_mp):
        n1_copies[o - 1].wait_recv()
    for o in range(1, n_mp):
        p_send[o - 1] = project(mp_peer[o])
        for i in range(batches):
            rows = slice(i * mid, (i + 1) * mid)
            cp = remote(p_send.at[o - 1, rows], p_recv.at[o - 1, rows],
                        p_ss.at[o, i], p_rs.at[o, i], (d, mp_peer[o]))
            cp.start()
            p_copies[o, i] = cp

    inv2, mix, n2s, hot = [], [], [], []
    for i in range(batches):
        cnt = column(ids_ref[2 * fan + 1, i : i + 1, :tgt])
        inv2.append(1.0 / cnt)
        n2 = counts_matrix(ids_ref[fan + 1 : 2 * fan + 1, i, :tgt], ids_ref[2 * fan + 1, i : i + 1, :tgt], mid, jnp.zeros((mid, tgt), F32))
        n2s.append(n2.astype(BF16))
        r = lax.broadcasted_iota(jnp.int32, (tgt, mid), 0)
        c = lax.broadcasted_iota(jnp.int32, (tgt, mid), 1)
        both = jnp.concatenate([jnp.where(r == c, 1.0, 0.0), n2], axis=0)
        mix.append(jnp.concatenate([both, both], axis=0).astype(BF16))
        lab = column(ids_ref[2 * fan + 2, i : i + 1, :tgt])
        lane = lax.broadcasted_iota(jnp.int32, (tgt, classes), 1).astype(F32)
        hot.append(jnp.where(lane == lab, 1.0, 0.0))
    dl_s[...] = jnp.zeros(dl_s.shape, F32)

    q_copies = {}
    bias_sum = jnp.zeros((1, width), F32)
    for i in range(batches):
        rows = slice(i * mid, (i + 1) * mid)
        total = p_own[rows, :]
        for o in range(1, n_mp):
            p_copies[o, i].wait_recv()
            total = total + p_recv[o - 1, rows, :]
        pre = bias_ref[...] + total * inv1[i]
        hidden = jnp.maximum(pre, 0.0).astype(BF16)
        top = hidden[:tgt]
        mean = (jnp.dot(n2s[i], hidden, preferred_element_type=F32) * inv2[i]).astype(BF16)
        logits = (lax.dot_general(top, sw_ref[...], COLS1, preferred_element_type=F32)
                  + lax.dot_general(mean, nw_ref[...], COLS1, preferred_element_type=F32))
        e = jnp.exp(logits - jnp.max(logits, axis=1, keepdims=True))
        probs = e / jnp.sum(e, axis=1, keepdims=True)
        dl = (probs - hot[i]) * scale
        here = slice(i * tgt, (i + 1) * tgt)
        dl_s[here, :classes] = dl
        hid_s[here, :] = top
        nm_s[here, :] = mean
        dlb = dl.astype(BF16)
        back_self = jnp.dot(dlb, sw_ref[...], preferred_element_type=F32)
        back_mean = jnp.dot(dlb, nw_ref[...], preferred_element_type=F32) * inv2[i]
        high, low = split(jnp.concatenate([back_self, back_mean], axis=0))
        grad_hidden = lax.dot_general(mix[i], jnp.concatenate([high, low], axis=0), ROWS0,
                                      preferred_element_type=F32)
        grad_pre = jnp.where(pre > 0, grad_hidden, 0.0)
        bias_sum = bias_sum + jnp.sum(grad_pre, axis=0, keepdims=True)
        gq[m, rows, :] = (grad_pre * inv1[i]).astype(BF16)
        for o in range(1, n_mp):
            cp = remote(gq.at[m, rows], gq.at[m, rows], q_ss.at[o, i], q_rs.at[o, i],
                        (d, mp_peer[o]))
            cp.start()
            q_copies[o, i] = cp

    dlb = dl_s[...].astype(BF16)
    own = lax.dot_general(dlb, hid_s[...], ROWS0, preferred_element_type=F32)
    neigh = lax.dot_general(dlb, nm_s[...], ROWS0, preferred_element_type=F32)
    row = lax.broadcasted_iota(jnp.int32, own.shape, 0)
    own = jnp.where(row == classes, bias_sum, own)
    everything = [own, neigh]
    if stot > 2 * cpad:
        everything.append(jnp.zeros((stot - 2 * cpad, width), F32))
    part_s[...] = jnp.concatenate(everything, axis=0).astype(BF16).reshape(part_s.shape)

    def chain(ci, part, prefix):
        plan, base = plans[ci], bases[ci]
        ag = bufs[bases[ci + 1] - 1]
        cur = part
        for at, (k, kind, f, w) in enumerate(plan):
            recv = bufs[base + 2 * at]
            copies = []
            for o in range(1, f):
                other, who = dp_peer(k, o)
                if kind == "all":
                    src, dst = cur, recv.at[digit[k]]
                else:
                    src, dst = cur.at[other], recv.at[o - 1]
                cp = remote(src, dst, st_ss.at[ci, k, o], st_rs.at[ci, k, o], who)
                cp.start()
                copies.append(cp)
            if kind == "all":
                recv[digit[k]] = cur[...]
            sends.extend(copies)
            yield
            for cp in copies:
                cp.wait_recv()
            if kind == "all":
                acc = recv[0].astype(F32)
                for j in range(1, f):
                    acc = acc + recv[j].astype(F32)
            else:
                acc = cur[digit[k]].astype(F32)
                for o in range(1, f):
                    acc = acc + recv[o - 1].astype(F32)
                prefix = prefix + (digit[k],)
            acc = acc.astype(BF16)
            if at == len(plan) - 1:
                ag[prefix] = acc
            else:
                nxt = bufs[base + 2 * at + 1]
                following = plan[at + 1]
                if following[1] == "col":
                    step = following[3]
                    for j in range(following[2]):
                        nxt[j] = acc[:, j * step : (j + 1) * step]
                else:
                    nxt[...] = acc.reshape(nxt.shape)
                cur = nxt
        for k, kind, f, w in reversed(plan):
            if kind == "all":
                continue
            copies = []
            for o in range(1, f):
                cp = remote(ag.at[prefix], ag.at[prefix], ag_ss.at[ci, k, o], ag_rs.at[ci, k, o],
                            dp_peer(k, o)[1])
                cp.start()
                copies.append(cp)
            sends.extend(copies)
            prefix = prefix[:-1]
            yield
            for cp in copies:
                cp.wait_recv()

    def spread(ci, out, row0):
        ag = bufs[bases[ci + 1] - 1]
        kept = [(kind, f) for k, kind, f, w in plans[ci] if kind != "all"]
        half, w = ag.shape[-2:]
        for at in itertools.product(*[range(f) for kind, f in kept]):
            row = col = 0
            for (kind, f), j in zip(kept, at):
                if kind == "row":
                    row = row * f + j
                else:
                    col = col * f + j
            top = row0 + row * half
            out[top : top + half, col * w : (col + 1) * w] = ag[at]

    def s_chain():
        yield from chain(0, part_s, ())
        spread(0, s_out, 0)

    def g_chain(ci, row0):
        rows = chunks[ci]
        part = part_g.at[ci - 1]
        part[...] = jnp.dot(
            zb[row0 : row0 + rows, :], gall, preferred_element_type=F32
        ).astype(BF16).reshape(part.shape)
        yield from chain(ci, part, ())
        spread(ci, g_out, row0)

    live = [s_chain()]
    next(live[0])
    for cp in q_copies.values():
        cp.wait_recv()
    gall = gq[...].reshape(n_mp * batches * mid, width)
    row0 = 0
    for ci in range(1, len(chunks)):
        gen = g_chain(ci, row0)
        next(gen)
        live.append(gen)
        row0 += chunks[ci]
    while live:
        for gen in list(live):
            try:
                next(gen)
            except StopIteration:
                live.remove(gen)

    for cp in n1_copies + list(p_copies.values()) + list(q_copies.values()) + sends:
        cp.wait_send()


def local(
    n_dp, n_mp,
    features, proj_weight, bias_first, self_weight, neigh_weight,
    first_neighbours, first_counts, second_neighbours, second_counts, labels,
):
    batches, _, depth = features.shape
    width = proj_weight.shape[1]
    mid = first_neighbours.shape[1]
    loc = features.shape[1] // n_mp
    tgt = labels.shape[1]
    classes = self_weight.shape[1]
    scale = 1.0 / math.sqrt(batches * tgt * n_dp * n_mp)
    fs = factors_of(n_dp)
    cpad = round_up(classes + 1, TILE)
    stot = round_up(2 * cpad, TILE * fs[0] * n_mp)
    parts = 3
    chunks = [stot] + [depth // parts] * parts
    n_st = len(fs)

    plans = [plan_of(fs, width, n_mp)] + [plan_of(fs, width, 1)] * parts
    bufs = []
    for plan, rows in zip(plans, chunks):
        for at, (k, kind, f, w) in enumerate(plan):
            if kind == "row":
                rows //= f
            bufs.append(pltpu.VMEM((f if kind == "all" else f - 1, rows, w), BF16))
            if at == len(plan) - 1:
                lead = tuple(f for k, kind, f, w in plan if kind != "all")
                bufs.append(pltpu.VMEM((*lead, rows, w), BF16))
            else:
                _, then, g, left = plan[at + 1]
                if then == "row":
                    bufs.append(pltpu.VMEM((g, rows // g, left), BF16))
                elif then == "col":
                    bufs.append(pltpu.VMEM((g, rows, left), BF16))
                else:
                    bufs.append(pltpu.VMEM((rows, left), BF16))
    peers = n_mp - 1
    most = max(*fs, n_mp)
    dma = pltpu.SemaphoreType.DMA
    stage = (len(chunks), n_st + 1, most)
    scratch = [
        pltpu.VMEM((n_mp, batches * mid, loc), BF16),
        pltpu.VMEM((depth, n_mp * batches * mid), BF16),
        pltpu.VMEM((batches * mid, width), F32),
        pltpu.VMEM((peers, batches * mid, width), F32),
        pltpu.VMEM((peers, batches * mid, width), F32),
        pltpu.VMEM((n_mp, batches * mid, width), BF16),
        pltpu.VMEM((batches * tgt, cpad), F32),
        pltpu.VMEM((batches * tgt, width), BF16),
        pltpu.VMEM((batches * tgt, width), BF16),
        pltpu.VMEM((parts, fs[0], depth // parts // fs[0], width), BF16),
        pltpu.VMEM((fs[0], stot // fs[0], width), BF16),
        *bufs,
        dma((n_mp,)), dma((n_mp,)),
        dma((n_mp, batches)), dma((n_mp, batches)),
        dma((n_mp, batches)), dma((n_mp, batches)),
        dma(stage), dma(stage), dma(stage), dma(stage),
    ]
    second = jnp.concatenate(
        [second_neighbours.transpose(2, 0, 1), second_counts[None], labels[None]], axis=0
    )
    ids = jnp.concatenate(
        [first_neighbours.transpose(2, 0, 1), first_counts[None],
         jnp.pad(second, ((0, 0), (0, 0), (0, mid - tgt)))], axis=0
    )
    vmem = pl.BlockSpec(memory_space=pltpu.VMEM)
    g, s = pl.pallas_call(
        functools.partial(kernel, (n_mp, n_dp, scale, fs, plans, chunks, tgt)),
        out_shape=(
            jax.ShapeDtypeStruct((depth, width), BF16),
            jax.ShapeDtypeStruct((stot, width), BF16),
        ),
        in_specs=[vmem] * 6,
        out_specs=(vmem, vmem),
        scratch_shapes=scratch,
        compiler_params=pltpu.CompilerParams(
            collective_id=0, has_side_effects=True, vmem_limit_bytes=40 * 1024 * 1024
        ),
    )(
        features, proj_weight, bias_first.reshape(1, width), self_weight.T, neigh_weight.T,
        ids,
    )
    return (
        g.astype(F32),
        s[:classes].T.astype(F32),
        s[cpad : cpad + classes].T.astype(F32),
        s[classes].astype(F32),
    )


def solution(mesh):
    placed = (
        P(None, "dp", "mp"),
        P("mp", None),
        P(),
        P(),
        P(),
        P(None, ("dp", "mp"), None),
        P(None, ("dp", "mp")),
        P(None, ("dp", "mp"), None),
        P(None, ("dp", "mp")),
        P(None, ("dp", "mp")),
    )
    body = functools.partial(local, mesh.shape["dp"], mesh.shape["mp"])
    return jax.shard_map(
        body, mesh=mesh, in_specs=placed, out_specs=(P("mp", None), P(), P(), P()), check_vma=False
    )
```
